128 devices in a mesh: dp: 32 (over y, x, core), tensor: 4 (over z).
Axes of the slice: x: 4, y: 4, z: 4, core: 2. Of those that a mesh axis runs over, the one named last changes fastest.
Arguments:
- layer_input: bfloat16 [32768, 2560], P('dp', 'tensor'), may hold values from -6 to 6
- norm_gain: float32 [2560], replicated, may hold values from 0.25 to 1.75
- shift_mix: float32 [2560], replicated, may hold values from 0 to 1
- key_weight: bfloat16 [2560, 5120], P(None, 'tensor'), may hold values from -0.125 to 0.125
- value_weight: bfloat16 [5120, 2560], P('tensor'), may hold values from -0.078125 to 0.078125
- key_left: bfloat16 [2048, 2560], P('dp'), may hold values from -6 to 6
- key_right: bfloat16 [2048, 5120], P('dp', 'tensor'), may hold values from -6 to 6
- value_left: bfloat16 [2048, 5120], P('dp', 'tensor'), may hold values from -6 to 6
- value_right: bfloat16 [2048, 2560], P('dp'), may hold values from -6 to 6
- fitness_rank: int32 [2048], P('dp'), may hold values from 0 to 2047, each once
Outputs:
- layer_output: bfloat16 [32768, 2560], P('dp', 'tensor')
- key_update: float32 [2560, 5120], P('dp', 'tensor')
- value_update: float32 [5120, 2560], P('tensor', 'dp')
The draws below stay inside these ranges and needn't reach their ends.
Inputs may be any that keep to these rules, and one draw needn't show every extreme that they name: `fitness_rank`: every value of 0 to 2047 appears once.
All inputs are finite; a program needn't handle non-finite values.
Results may differ from the reference program's by a relative error of at most 0.006.
Values may be sent and summed in bfloat16 or wider, within the bound.
No kernel may reach another device: no remote copies, remote signals or barrier semaphores. Data moves between devices by JAX's collectives and lax.ppermute only.
A program may use at most 192 MiB of HBM per device.

```python
import math
import jax
import jax.numpy as jnp
from jax import lax

D = 2560
FFW = 5120
PROMPT_LEN = 16
MEMBERS = 2048
ROWS = 32768


def level_of(rng, shape, cuts, least, top_value):
    factor_of, own = 1.0, jax.random.fold_in(rng, 6)
    for position, blocks in cuts:
        heights = jnp.exp(jax.random.uniform(jax.random.fold_in(own, position), (blocks,), jnp.float32, least / len(cuts), top_value / len(cuts)))
        factor_of = factor_of * jnp.repeat(heights, shape[position] // blocks).reshape([-1 if axis == position else 1 for axis in range(len(shape))])
    return factor_of


def scatter_about(own_key, shape, deviation, most, shards=(), held_as=jnp.bfloat16):
    entries = deviation * jax.random.normal(own_key, shape, jnp.float32)
    if shards:
        entries = entries * level_of(own_key, shape, shards, -0.22, 0.18)
    return jnp.clip(entries, -most, most).astype(held_as)


def setup_inputs(seed: int = 0) -> dict:
    streams_of = jax.random.split(jax.random.key(seed), 11)
    layer_input = scatter_about(streams_of[0], (ROWS, D), 1.0, 6.0, ((0, 32), (1, 4)))
    norm_gain = jnp.clip(1.0 + 0.15 * jax.random.normal(streams_of[1], (D,), jnp.float32), 0.25, 1.75)
    shift_mix = jnp.clip(jax.random.uniform(streams_of[2], (D,), jnp.float32, 0.0, 1.0), 0.0, 1.0)
    key_weight = scatter_about(streams_of[3], (D, FFW), D ** -0.5, 0.125, ((1, 4),))
    value_weight = scatter_about(streams_of[4], (FFW, D), FFW ** -0.5, 0.078125, ((0, 4),))
    key_left = scatter_about(streams_of[5], (MEMBERS, D), 1.0, 6.0, ((0, 32),))
    key_right = scatter_about(streams_of[6], (MEMBERS, FFW), 1.0, 6.0, ((0, 32), (1, 4)))
    value_left = scatter_about(streams_of[7], (MEMBERS, FFW), 1.0, 6.0, ((0, 32), (1, 4)))
    value_right = scatter_about(streams_of[8], (MEMBERS, D), 1.0, 6.0, ((0, 32),))
    fitness_rank = jax.random.permutation(streams_of[9], MEMBERS).astype(jnp.int32)
    return dict(layer_input=layer_input, norm_gain=norm_gain, shift_mix=shift_mix, key_weight=key_weight, value_weight=value_weight, key_left=key_left, key_right=key_right, value_left=value_left, value_right=value_right, fitness_rank=fitness_rank)


epsilon = 1e-05
sigma = 0.5

def forward_block(inputs, norm_gain, shift_mix, key_weight, value_weight):
    rows, lefts, rights, vlefts, vrights = inputs
    members = lefts.shape[0]
    values = rows.astype(jnp.float32)
    centre = lax.optimization_barrier(jnp.mean(values, axis=-1, keepdims=True))
    spread = lax.optimization_barrier(jnp.mean((values - centre) ** 2, axis=-1, keepdims=True))
    normed = (values - centre) * lax.rsqrt(spread + epsilon) * norm_gain
    grid = normed.reshape(members, PROMPT_LEN, D)
    previous = jnp.concatenate([jnp.zeros_like(grid[:, :1]), grid[:, :-1]], axis=1)
    mixed = (grid + (previous - grid) * shift_mix).astype(jnp.bfloat16)
    key_dots = jnp.einsum('mld,md->ml', mixed.astype(jnp.float32), lefts.astype(jnp.float32))
    preact = jnp.dot(mixed.reshape(-1, D), key_weight, preferred_element_type=jnp.float32).reshape(members, PROMPT_LEN, FFW)
    preact = preact + sigma / math.sqrt(D) * key_dots[..., None] * rights.astype(jnp.float32)[:, None, :]
    hidden = (jnp.maximum(preact, 0.0) ** 2).astype(jnp.bfloat16)
    value_dots = jnp.einsum('mlf,mf->ml', hidden.astype(jnp.float32), vlefts.astype(jnp.float32))
    output = jnp.dot(hidden.reshape(-1, FFW), value_weight, preferred_element_type=jnp.float32).reshape(members, PROMPT_LEN, D)
    output = output + sigma / math.sqrt(FFW) * value_dots[..., None] * vrights.astype(jnp.float32)[:, None, :]
    return output.astype(jnp.bfloat16).reshape(members * PROMPT_LEN, D)

def reference(layer_input, norm_gain, shift_mix, key_weight, value_weight, key_left, key_right, value_left, value_right, fitness_rank):
    block = math.gcd(MEMBERS, 64)
    blocks = MEMBERS // block
    inputs = (layer_input.reshape(blocks, block * PROMPT_LEN, D), key_left.reshape(blocks, block, D), key_right.reshape(blocks, block, FFW), value_left.reshape(blocks, block, FFW), value_right.reshape(blocks, block, D))
    outputs = lax.map(lambda part: forward_block(part, norm_gain, shift_mix, key_weight, value_weight), inputs)
    layer_output = outputs.reshape(ROWS, D)
    member_weight = (fitness_rank.astype(jnp.float32) / (MEMBERS - 1) - 0.5) / math.sqrt(MEMBERS)
    key_scaled = (key_left.astype(jnp.float32) * member_weight[:, None]).astype(jnp.bfloat16)
    key_update = jnp.dot(key_scaled.T, key_right, preferred_element_type=jnp.float32)
    value_scaled = (value_right.astype(jnp.float32) * member_weight[:, None]).astype(jnp.bfloat16)
    value_update = jnp.dot(value_left.T, value_scaled, preferred_element_type=jnp.float32)
    return (layer_output, key_update, value_update)
```

```python
import functools
import math

import jax
import jax.numpy as jnp
from jax import lax
from jax.experimental import pallas as pl
from jax.experimental.pallas import tpu as pltpu
from jax.sharding import PartitionSpec as P

D = 2560
FFW = 5120
PROMPT = 16
EPSILON = 1e-05
SIGMA = 0.5
KEY_FACTOR = SIGMA / math.sqrt(D)
VALUE_FACTOR = SIGMA / math.sqrt(FFW)
CHUNKS = 2
LN_ROWS = 64
MM_ROWS = 256
F_BLOCK = 256


def split_dots(dots):
    high = dots.astype(jnp.bfloat16)
    low = (dots - high.astype(jnp.float32)).astype(jnp.bfloat16)
    return high, low


def own_member(rows, members, first_row):
    row = lax.broadcasted_iota(jnp.int32, (rows, members), 0) + first_row
    member = lax.broadcasted_iota(jnp.int32, (rows, members), 1)
    return row // PROMPT == member


def mm(a, b):
    return jnp.dot(a, b, preferred_element_type=jnp.float32)


def mm_t(a, b):
    return lax.dot_general(a, b, (((1,), (1,)), ((), ())), preferred_element_type=jnp.float32)


def ffn_kernel(
    place,
    x0,
    x1,
    x2t,
    x2b,
    x3,
    gain,
    mix,
    kw,
    vw,
    kl,
    kr,
    vl,
    vr,
    o0,
    o1,
    o2t,
    o2b,
    o3,
    mixed,
    acc,
    kdots,
    vdots,
):
    step = pl.program_id(0)
    steps = pl.num_programs(0)
    rows, width = x0.shape
    half = rows // 2
    members = kl.shape[0]
    z = place[0]

    def column(k):
        return pl.multiple_of(lax.rem(z + k, 4) * width, 128)

    def normalise(i, source2, offset2):
        first = pl.multiple_of(i * LN_ROWS, LN_ROWS)
        span = pl.ds(first, LN_ROWS)
        span2 = pl.ds(pl.multiple_of(first - offset2, LN_ROWS), LN_ROWS)
        pieces = [x0[span, :], x1[span, :], source2[span2, :], x3[span, :]]
        pieces = [p.astype(jnp.float32) for p in pieces]
        total = sum(jnp.sum(p, axis=-1, keepdims=True) for p in pieces)
        centre = total * (1.0 / D)
        pieces = [p - centre for p in pieces]
        spread = sum(jnp.sum(p * p, axis=-1, keepdims=True) for p in pieces) * (1.0 / D)
        scale = lax.rsqrt(spread + EPSILON)
        start = lax.broadcasted_iota(jnp.int32, (LN_ROWS, 1), 0) % PROMPT == 0
        for k, piece in enumerate(pieces):
            cols = pl.ds(column(k), width)
            normed = piece * scale * gain[:, cols]
            previous = jnp.where(start, 0.0, pltpu.roll(normed, 1, 0))
            mixed[span, cols] = (normed + (previous - normed) * mix[:, cols]).astype(jnp.bfloat16)

    @pl.when(step == 0)
    def _():
        lax.fori_loop(0, half // LN_ROWS, lambda i, _: (normalise(i, x2t, 0), 0)[1], 0)
        lax.fori_loop(half // LN_ROWS, rows // LN_ROWS, lambda i, _: (normalise(i, x2b, half), 0)[1], 0)

    def block(i, _):
        first = pl.multiple_of(i * MM_ROWS, MM_ROWS)
        span = pl.ds(first, MM_ROWS)
        rows_mixed = mixed[span, :]
        mine = own_member(MM_ROWS, members, first)

        @pl.when(step == 0)
        def _():
            kdots[span, :] = jnp.where(mine, mm_t(rows_mixed, kl[...]) * KEY_FACTOR, 0.0)

        high, low = split_dots(kdots[span, :])
        right = kr[...]
        preact = mm(rows_mixed, kw[...]) + (mm(high, right) + mm(low, right))
        hidden = jnp.square(jnp.maximum(preact, 0.0)).astype(jnp.bfloat16)
        dots = mm_t(hidden, vl[...])
        sums = mm(hidden, vw[...])

        @pl.when(step == 0)
        def _():
            vdots[span, :] = dots
            acc[span, :] = sums

        @pl.when(step > 0)
        def _():
            vdots[span, :] += dots
            acc[span, :] += sums

        return 0

    lax.fori_loop(0, rows // MM_ROWS, block, 0)

    @pl.when(step == steps - 1)
    def _():
        for first in range(0, rows, MM_ROWS):
            span = pl.ds(first, MM_ROWS)
            mine = own_member(MM_ROWS, members, first)
            high, low = split_dots(jnp.where(mine, vdots[span, :] * VALUE_FACTOR, 0.0))

            def piece(k):
                cols = pl.ds(column(k), width)
                right = vr[:, cols]
                return acc[span, cols] + (mm(high, right) + mm(low, right))

            o0[span, :] = piece(0)
            o1[span, :] = piece(1).astype(jnp.bfloat16)
            o3[span, :] = piece(3).astype(jnp.bfloat16)
            target2, first2 = (o2t, first) if first < half else (o2b, first - half)
            target2[pl.ds(first2, MM_ROWS), :] = piece(2).astype(jnp.bfloat16)


def ffn(place, pieces, gain, mix, kw, vw, kl, kr, vl, vr):
    rows, width = pieces[0].shape
    members, hidden = kr.shape
    half = rows // 2

    def whole(shape):
        return pl.BlockSpec(shape, lambda f, s: (0,) * len(shape))

    out_shapes = [
        jax.ShapeDtypeStruct((rows, width), jnp.float32),
        jax.ShapeDtypeStruct((rows, width), jnp.bfloat16),
        jax.ShapeDtypeStruct((half, width), jnp.bfloat16),
        jax.ShapeDtypeStruct((half, width), jnp.bfloat16),
        jax.ShapeDtypeStruct((rows, width), jnp.bfloat16),
    ]
    return pl.pallas_call(
        ffn_kernel,
        out_shape=out_shapes,
        grid_spec=pltpu.PrefetchScalarGridSpec(
            num_scalar_prefetch=1,
            grid=(hidden // F_BLOCK,),
            in_specs=[whole(p.shape) for p in pieces]
            + [
                whole((1, D)),
                whole((1, D)),
                pl.BlockSpec((D, F_BLOCK), lambda f, s: (0, f)),
                pl.BlockSpec((F_BLOCK, D), lambda f, s: (f, 0)),
                whole((members, D)),
                pl.BlockSpec((members, F_BLOCK), lambda f, s: (0, f)),
                pl.BlockSpec((members, F_BLOCK), lambda f, s: (0, f)),
                whole((members, D)),
            ],
            out_specs=[whole(s.shape) for s in out_shapes],
            scratch_shapes=[
                pltpu.VMEM((rows, D), jnp.bfloat16),
                pltpu.VMEM((rows, D), jnp.float32),
                pltpu.VMEM((rows, members), jnp.float32),
                pltpu.VMEM((rows, members), jnp.float32),
            ],
        ),
        compiler_params=pltpu.CompilerParams(
            dimension_semantics=("arbitrary",), vmem_limit_bytes=48 * 1024 * 1024
        ),
        cost_estimate=pl.CostEstimate(
            flops=4 * rows * D * hidden,
            bytes_accessed=4 * D * hidden + 8 * rows * D,
            transcendentals=rows,
        ),
    )(place, *pieces, gain, mix, kw, vw, kl, kr, vl, vr)


def shift(array, by):
    return lax.ppermute(array, "tensor", [(i, (i + by) % 4) for i in range(4)])


def local(
    layer_input,
    norm_gain,
    shift_mix,
    key_weight,
    value_weight,
    key_left,
    key_right,
    value_left,
    value_right,
    fitness_rank,
):
    members = key_left.shape[0]
    devices = lax.axis_size("dp")
    hidden = key_weight.shape[1]
    place = lax.axis_index("tensor").astype(jnp.int32).reshape(1)
    gain, mix = norm_gain.reshape(1, D), shift_mix.reshape(1, D)
    rows = layer_input.shape[0] // CHUNKS
    half = rows // 2

    gathered = []
    for c in range(CHUNKS):
        own = layer_input[c * rows : (c + 1) * rows]
        from_left, from_right = shift(own, 1), shift(own, -1)
        far_top = shift(from_left[:half], 1)
        far_bottom = shift(from_right[half:], -1)
        gathered.append([own, from_right, far_top, far_bottom, from_left])

    rights = lax.all_gather(
        jnp.concatenate([key_right, value_left], axis=1), "dp", axis=0, tiled=True
    )
    total_members = members * devices
    member_weight = (fitness_rank.astype(jnp.float32) / (total_members - 1) - 0.5) / math.sqrt(
        total_members
    )

    def scaled(factor):
        product = (factor.astype(jnp.float32) * member_weight[:, None]).astype(jnp.bfloat16)
        return product.reshape(members, devices, -1).transpose(1, 0, 2)

    lefts = jnp.concatenate([scaled(key_left), scaled(value_right)], axis=2)
    lefts = lax.all_to_all(lefts, "dp", split_axis=0, concat_axis=0, tiled=True)
    lefts = lefts.reshape(total_members, -1)
    share = lefts.shape[1] // 2
    contract = (((0,), (0,)), ((), ()))
    key_update = lax.dot_general(
        lefts[:, :share], rights[:, :hidden], contract, preferred_element_type=jnp.float32
    )
    value_update = lax.dot_general(
        rights[:, hidden:], lefts[:, share:], contract, preferred_element_type=jnp.float32
    )

    outputs = []
    for c in range(CHUNKS):
        part = slice(c * rows // PROMPT, (c + 1) * rows // PROMPT)
        own, right, far_top, far_bottom, left = ffn(
            place,
            gathered[c],
            gain,
            mix,
            key_weight,
            value_weight,
            key_left[part],
            key_right[part],
            value_left[part],
            value_right[part],
        )
        via_left, via_right = shift(far_top, 1), shift(far_bottom, -1)
        right = jnp.concatenate([right[:half] + via_left, right[half:]], axis=0)
        left = jnp.concatenate([left[:half], left[half:] + via_right], axis=0)
        got = shift(right, 1).astype(jnp.float32) + shift(left, -1).astype(jnp.float32)
        outputs.append((own + got).astype(jnp.bfloat16))
    return (jnp.concatenate(outputs, axis=0), key_update, value_update)


def solution(mesh):
    placed = (
        P("dp", "tensor"),
        P(),
        P(),
        P(None, "tensor"),
        P("tensor", None),
        P("dp", None),
        P("dp", "tensor"),
        P("dp", "tensor"),
        P("dp", None),
        P("dp"),
    )
    return jax.shard_map(
        local,
        mesh=mesh,
        in_specs=placed,
        out_specs=(P("dp", "tensor"), P("dp", "tensor"), P("tensor", "dp")),
        check_vma=False,
    )
```

```python
import functools
import math

import jax
import jax.numpy as jnp
from jax import lax
from jax.experimental import pallas as pl
from jax.experimental.pallas import tpu as pltpu
from jax.sharding import PartitionSpec as P

D = 2560
FFW = 5120
PROMPT = 16
EPSILON = 1e-05
SIGMA = 0.5
KEY_FACTOR = SIGMA / math.sqrt(D)
VALUE_FACTOR = SIGMA / math.sqrt(FFW)
CHUNKS = 2
LN_ROWS = 64
F_BLOCK = 640


def mm(a, b):
    return jnp.dot(a, b, preferred_element_type=jnp.float32)


def per_member(array, rows):
    members, width = array.shape
    wide = jnp.broadcast_to(array.astype(jnp.float32)[:, None, :], (members, PROMPT, width))
    return wide.reshape(rows, width)


def ffn_kernel(
    place,
    x0,
    x1t,
    x2t,
    x3t,
    x1b,
    x2b,
    x3b,
    keep,
    pass_on,
    kw_hbm,
    vw_hbm,
    kl,
    kr,
    vl,
    vr,
    o0,
    o1t,
    o2t,
    o3t,
    o1b,
    o2b,
    o3b,
    kw,
    vw,
    mixed,
    hidden,
    kdots,
    sems,
):
    rows, width = x0.shape
    half = rows // 2
    units = kw.shape[1]
    z = place[0]
    key_copy = pltpu.make_async_copy(kw_hbm, kw, sems.at[0])
    value_copy = pltpu.make_async_copy(vw_hbm, vw, sems.at[1])
    key_copy.start()
    value_copy.start()

    def column(k):
        return pl.multiple_of(lax.rem(z + k, 4) * width, 128)

    def normalise(i, sub, sources, offset):
        first = pl.multiple_of(i * 128 + sub * LN_ROWS, LN_ROWS)
        span = pl.ds(first, LN_ROWS)
        from_half = pl.ds(pl.multiple_of(first - offset, LN_ROWS), LN_ROWS)
        group = pl.ds(pl.multiple_of(i * 8, 8), 8)
        ours = slice(sub * LN_ROWS // PROMPT, (sub + 1) * LN_ROWS // PROMPT)
        pieces = [x0[span, :]] + [source[from_half, :] for source in sources]
        pieces = [p.astype(jnp.float32) for p in pieces]
        total = sum(jnp.sum(p, axis=-1, keepdims=True) for p in pieces)
        centre = total * (1.0 / D)
        pieces = [p - centre for p in pieces]
        spread = sum(jnp.sum(p * p, axis=-1, keepdims=True) for p in pieces) * (1.0 / D)
        scale = lax.rsqrt(spread + EPSILON)
        later = lax.broadcasted_iota(jnp.int32, (LN_ROWS, 1), 0) % PROMPT != 0
        dots = 0.0
        for k, piece in enumerate(pieces):
            cols = pl.ds(column(k), width)
            normed = piece * scale
            before = pltpu.roll(normed * pass_on[:, cols], 1, 0)
            piece = normed * keep[:, cols] + jnp.where(later, before, 0.0)
            piece = piece.astype(jnp.bfloat16)
            mixed[span, cols] = piece
            left = per_member(kl[group, cols][ours], LN_ROWS)
            dots += jnp.sum(piece.astype(jnp.float32) * left, axis=-1, keepdims=True)
        kdots[span, :] = dots * KEY_FACTOR

    def normalise_group(sources, offset, i, carry):
        for sub in range(128 // LN_ROWS):
            normalise(i, sub, sources, offset)
        return carry

    top = functools.partial(normalise_group, (x1t, x2t, x3t), 0)
    bottom = functools.partial(normalise_group, (x1b, x2b, x3b), half)
    lax.fori_loop(0, half // 128, top, 0)
    lax.fori_loop(half // 128, rows // 128, bottom, 0)

    key_copy.wait()
    vdots = 0.0
    for first in range(0, units, F_BLOCK):
        cols = pl.ds(first, F_BLOCK)
        preact = mm(mixed[...], kw[:, cols]) + kdots[...] * per_member(kr[:, cols], rows)
        block = jnp.square(jnp.maximum(preact, 0.0)).astype(jnp.bfloat16)
        hidden[:, cols] = block
        left = per_member(vl[:, cols], rows)
        vdots += jnp.sum(block.astype(jnp.float32) * left, axis=-1, keepdims=True)
    vdots = vdots * VALUE_FACTOR

    value_copy.wait()

    def piece(k):
        cols = pl.ds(column(k), width)
        return mm(hidden[...], vw[:, cols]) + vdots * per_member(vr[:, cols], rows)

    for k, top, bottom in ((2, o2t, o2b), (1, o1t, o1b), (3, o3t, o3b)):
        sums = piece(k).astype(jnp.bfloat16)
        top[...] = sums[:half]
        bottom[...] = sums[half:]
    o0[...] = piece(0)


def ffn(place, pieces, gain, mix, kw, vw, kl, kr, vl, vr):
    rows, width = pieces[0].shape
    units = kr.shape[1]
    half = rows // 2
    vmem = pl.BlockSpec(memory_space=pltpu.VMEM)
    hbm = pl.BlockSpec(memory_space=pl.ANY)
    part = jax.ShapeDtypeStruct((half, width), jnp.bfloat16)
    out_shapes = [jax.ShapeDtypeStruct((rows, width), jnp.float32)] + [part] * 6
    return pl.pallas_call(
        ffn_kernel,
        out_shape=out_shapes,
        in_specs=[pl.BlockSpec(memory_space=pltpu.SMEM)] + [vmem] * 9 + [hbm] * 2 + [vmem] * 4,
        out_specs=[vmem] * 7,
        scratch_shapes=[
            pltpu.VMEM((D, units), jnp.bfloat16),
            pltpu.VMEM((units, D), jnp.bfloat16),
            pltpu.VMEM((rows, D), jnp.bfloat16),
            pltpu.VMEM((rows, units), jnp.bfloat16),
            pltpu.VMEM((rows, 1), jnp.float32),
            pltpu.SemaphoreType.DMA((2,)),
        ],
        compiler_params=pltpu.CompilerParams(vmem_limit_bytes=50 * 1024 * 1024),
        cost_estimate=pl.CostEstimate(
            flops=4 * rows * D * units,
            bytes_accessed=4 * D * units + 8 * rows * D,
            transcendentals=rows,
        ),
    )(place, *pieces, gain * (1.0 - mix), gain * mix, kw, vw, kl.astype(jnp.float32), kr, vl, vr)


def shift(array, by):
    return lax.ppermute(array, "tensor", [(i, (i + by) % 4) for i in range(4)])


def local(
    layer_input,
    norm_gain,
    shift_mix,
    key_weight,
    value_weight,
    key_left,
    key_right,
    value_left,
    value_right,
    fitness_rank,
):
    members = key_left.shape[0]
    devices = lax.axis_size("dp")
    hidden = key_weight.shape[1]
    place = lax.axis_index("tensor").astype(jnp.int32).reshape(1)
    gain, mix = norm_gain.reshape(1, D), shift_mix.reshape(1, D)
    rows = layer_input.shape[0] // CHUNKS
    half = rows // 2

    gathered = []
    for c in range(CHUNKS):
        own = layer_input[c * rows : (c + 1) * rows]
        if gathered:
            own, gathered[-1][4], gathered[-1][1] = lax.optimization_barrier(
                (own, gathered[-1][4], gathered[-1][1])
            )
        top, bottom = own[:half], own[half:]
        left_top, right_bottom = shift(top, 1), shift(bottom, -1)
        right_top, left_bottom = shift(top, -1), shift(bottom, 1)
        far_top, far_bottom = shift(left_top, 1), shift(right_bottom, -1)
        gathered.append(
            [own, right_top, far_top, left_top, right_bottom, far_bottom, left_bottom]
        )

    total_members = members * devices
    member_weight = (fitness_rank.astype(jnp.float32) / (total_members - 1) - 0.5) / math.sqrt(
        total_members
    )

    def scaled(factor):
        product = (factor.astype(jnp.float32) * member_weight[:, None]).astype(jnp.bfloat16)
        return product.reshape(members, devices, -1).transpose(1, 0, 2)

    lefts = jnp.concatenate([scaled(key_left), scaled(value_right)], axis=2)
    lefts = lax.all_to_all(lefts, "dp", split_axis=0, concat_axis=0, tiled=True)
    place_later, lefts = lax.optimization_barrier((place, lefts))
    lefts = lefts.reshape(total_members, -1)
    rights = lax.all_gather(
        jnp.concatenate([key_right, value_left], axis=1), "dp", axis=0, tiled=True
    )
    share = lefts.shape[1] // 2
    contract = (((0,), (0,)), ((), ()))
    key_update = lax.dot_general(
        lefts[:, :share], rights[:, :hidden], contract, preferred_element_type=jnp.float32
    )
    value_update = lax.dot_general(
        rights[:, hidden:], lefts[:, share:], contract, preferred_element_type=jnp.float32
    )

    outputs = []
    for c in range(CHUNKS):
        part = slice(c * rows // PROMPT, (c + 1) * rows // PROMPT)
        own, right_top, far_top, left_top, right_bottom, far_bottom, left_bottom = ffn(
            place if c == 0 else place_later,
            gathered[c],
            gain,
            mix,
            key_weight,
            value_weight,
            key_left[part],
            key_right[part],
            value_left[part],
            value_right[part],
        )
        via_left, via_right = shift(far_top, 1), shift(far_bottom, -1)
        from_left_bottom, from_right_top = shift(right_bottom, 1), shift(left_top, -1)
        from_left_top = shift(right_top + via_left, 1)
        from_right_bottom = shift(left_bottom + via_right, -1)
        if c == CHUNKS - 1:
            own, key_update, value_update = lax.optimization_barrier(
                (own, key_update, value_update)
            )
        for mine, one, two in (
            (own[:half], from_left_top, from_right_top),
            (own[half:], from_left_bottom, from_right_bottom),
        ):
            total = mine + (one.astype(jnp.float32) + two.astype(jnp.float32))
            outputs.append(total.astype(jnp.bfloat16))
    return (jnp.concatenate(outputs, axis=0), key_update, value_update)


def solution(mesh):
    placed = (
        P("dp", "tensor"),
        P(),
        P(),
        P(None, "tensor"),
        P("tensor", None),
        P("dp", None),
        P("dp", "tensor"),
        P("dp", "tensor"),
        P("dp", None),
        P("dp"),
    )
    return jax.shard_map(
        local,
        mesh=mesh,
        in_specs=placed,
        out_specs=(P("dp", "tensor"), P("dp", "tensor"), P("tensor", "dp")),
        check_vma=False,
    )
```

```python
import functools
import math

import jax
import jax.numpy as jnp
from jax import lax
from jax.experimental import pallas as pl
from jax.experimental.pallas import tpu as pltpu
from jax.sharding import Mesh, PartitionSpec as P

D = 2560
FFW = 5120
MEMBERS = 2048
PROMPT = 16
EPSILON = 1e-05
SIGMA = 0.5
KEY_FACTOR = SIGMA / math.sqrt(D)
VALUE_FACTOR = SIGMA / math.sqrt(FFW)
LN_ROWS = 64
F_BLOCK = 640
LANES = 128
MIB = 1024 * 1024

VMEM = pl.BlockSpec(memory_space=pltpu.VMEM)
SMEM = pl.BlockSpec(memory_space=pltpu.SMEM)
ANY = pl.BlockSpec(memory_space=pl.ANY)


def mm(a, b):
    return jnp.dot(a, b, preferred_element_type=jnp.float32)


def per_member(array, rows):
    members, width = array.shape
    wide = jnp.broadcast_to(array.astype(jnp.float32)[:, None, :], (members, PROMPT, width))
    return wide.reshape(rows, width)


def ffn_kernel(place, x0, *refs):
    pieces, refs = refs[:-20], refs[-20:]
    keep, pass_on, kw_hbm, vw_hbm, kl, kr, vl, vr, _, *refs = refs
    own, to_right, to_left, right_top, left_bottom, kw, vw, mixed, hidden, kdots, sems = refs
    rows, width = x0.shape
    half = rows // 2
    units = kw.shape[1]
    z = place[0]
    key_copy = pltpu.make_async_copy(kw_hbm, kw, sems.at[0])
    value_copy = pltpu.make_async_copy(vw_hbm, vw, sems.at[1])
    key_copy.start()
    value_copy.start()

    def column(k):
        return pl.multiple_of(lax.rem(z + k, 4) * width, 128)

    def normalise(i, sub, sources):
        first = pl.multiple_of(i * 128 + sub * LN_ROWS, LN_ROWS)
        span = pl.ds(first, LN_ROWS)
        group = pl.ds(pl.multiple_of(i * 8, 8), 8)
        ours = slice(sub * LN_ROWS // PROMPT, (sub + 1) * LN_ROWS // PROMPT)
        values = [x0[span, :]]
        for source, offset in sources:
            values.append(source[pl.ds(pl.multiple_of(first - offset, LN_ROWS), LN_ROWS), :])
        values = [v.astype(jnp.float32) for v in values]
        centre = sum(jnp.sum(v, axis=-1, keepdims=True) for v in values) * (1.0 / D)
        values = [v - centre for v in values]
        spread = sum(jnp.sum(v * v, axis=-1, keepdims=True) for v in values) * (1.0 / D)
        scale = lax.rsqrt(spread + EPSILON)
        later = lax.broadcasted_iota(jnp.int32, (LN_ROWS, 1), 0) % PROMPT != 0
        dots = 0.0
        for k, value in enumerate(values):
            cols = pl.ds(column(k), width)
            normed = value * scale
            before = pltpu.roll(normed * pass_on[:, cols], 1, 0)
            block = normed * keep[:, cols] + jnp.where(later, before, 0.0)
            block = block.astype(jnp.bfloat16)
            mixed[span, cols] = block
            left = per_member(kl[group, cols][ours], LN_ROWS)
            dots += jnp.sum(block.astype(jnp.float32) * left, axis=-1, keepdims=True)
        kdots[span, :] = dots * KEY_FACTOR

    def normalise_group(sources, i, carry):
        for sub in range(128 // LN_ROWS):
            normalise(i, sub, sources)
        return carry

    groups = rows // 128
    if len(pieces) == 4:
        right, left, far_top, far_bottom = pieces
        top, bottom = [(right, 0), (far_top, 0), (left, 0)], [(right, 0), (far_bottom, half), (left, 0)]
    else:
        near, far = pieces[:4], pieces[4:]
        top = [(near[0], 0), (far[0], 0), (near[1], 0)]
        bottom = [(near[2], half), (far[1], half), (near[3], half)]
    lax.fori_loop(0, groups // 2, functools.partial(normalise_group, top), 0)
    lax.fori_loop(groups // 2, groups, functools.partial(normalise_group, bottom), 0)

    key_copy.wait()
    vdots = 0.0
    for first in range(0, units, F_BLOCK):
        cols = pl.ds(first, F_BLOCK)
        preact = mm(mixed[...], kw[:, cols]) + kdots[...] * per_member(kr[:, cols], rows)
        block = jnp.square(jnp.maximum(preact, 0.0)).astype(jnp.bfloat16)
        hidden[:, cols] = block
        left = per_member(vl[:, cols], rows)
        vdots += jnp.sum(block.astype(jnp.float32) * left, axis=-1, keepdims=True)
    vdots = vdots * VALUE_FACTOR

    value_copy.wait()

    def sums(k):
        cols = pl.ds(column(k), width)
        return mm(hidden[...], vw[:, cols]) + vdots * per_member(vr[:, cols], rows)

    far = sums(2).astype(jnp.bfloat16)
    to_right[:half] = far[:half]
    to_left[half:] = far[half:]
    right = sums(1).astype(jnp.bfloat16)
    right_top[...] = right[:half]
    to_right[half:] = right[half:]
    left = sums(3).astype(jnp.bfloat16)
    to_left[:half] = left[:half]
    left_bottom[...] = left[half:]
    own[...] = sums(0)


def ffn(place, own, pieces, keep, pass_on, kw, vw, kl, kr, vl, vr, after):
    rows, width = own.shape
    units = kr.shape[1]
    half = rows // 2
    parts = [jax.ShapeDtypeStruct((n, width), jnp.bfloat16) for n in (rows, rows, half, half)]
    return pl.pallas_call(
        ffn_kernel,
        out_shape=[jax.ShapeDtypeStruct((rows, width), jnp.float32)] + parts,
        in_specs=[SMEM] + [VMEM] * (len(pieces) + 3) + [ANY] * 2 + [VMEM] * 4 + [ANY],
        out_specs=[VMEM] * 5,
        scratch_shapes=[
            pltpu.VMEM((D, units), jnp.bfloat16),
            pltpu.VMEM((units, D), jnp.bfloat16),
            pltpu.VMEM((rows, D), jnp.bfloat16),
            pltpu.VMEM((rows, units), jnp.bfloat16),
            pltpu.VMEM((rows, 1), jnp.float32),
            pltpu.SemaphoreType.DMA((2,)),
        ],
        compiler_params=pltpu.CompilerParams(vmem_limit_bytes=50 * MIB),
        cost_estimate=pl.CostEstimate(
            flops=8 * rows * D * units,
            bytes_accessed=4 * D * units + 8 * rows * D,
            transcendentals=rows,
        ),
    )(place, own, *pieces, keep, pass_on, kw, vw, kl, kr, vl, vr, after)


def prepare_kernel(place, weight, key_left, value_right, key_right, value_left, _, sent):
    core = place[0]
    rights = jnp.concatenate([key_right[...], value_left[...]], axis=0)
    scaled = [f[...].astype(jnp.float32) * weight[...] for f in (key_left, value_right)]
    lefts = jnp.concatenate([s.T for s in scaled], axis=1).astype(jnp.bfloat16)
    share = D // 32
    for x in range(4):
        for block in range(rights.shape[1] // LANES):
            rows = slice(4 * share + block * LANES, 4 * share + (block + 1) * LANES)
            sent[x, rows, :] = rights[:, block * LANES : (block + 1) * LANES]
        for c in range(2):
            first = jnp.where(core == c, 0, 4 * share + rights.shape[1])
            for y in range(4):
                start = ((y * 4 + x) * 2 + c) * share
                target = pl.ds(pl.multiple_of(first + y * share, 16), share)
                sent[x, target, :] = lefts[start : start + share]


def update_kernel(place, gathered, swapped, own, parts, sums):
    share, units = own.shape
    share //= 2
    lefts, rights = [], []
    for source, first_left, first_right in ((gathered, 0, 4 * share), (swapped, units, 0)):
        for x in range(4):
            lefts.append(source[x, first_left : first_left + 4 * share, :])
            blocks = range(first_right, first_right + units, LANES)
            rights.append(jnp.concatenate([source[x, b : b + LANES, :] for b in blocks], axis=1))
    rights = jnp.concatenate(rights, axis=0)
    lane = lax.broadcasted_iota(jnp.int32, lefts[0].shape, 1)
    for side in range(2):
        picked = [jnp.where((lane < LANES // 2) == (side == 0), b, 0.0) for b in lefts]
        total = mm(jnp.concatenate(picked, axis=1), rights)
        for y in range(4):
            sums[y, side * share : (side + 1) * share, :] = total[y * share : (y + 1) * share]
    own[...] = sums[place[0]]
    parts[...] = sums[...].astype(jnp.bfloat16)


def update_products(gathered, swapped, units):
    share = D // 16
    y = lax.axis_index("y").astype(jnp.int32).reshape(1)
    return pl.pallas_call(
        update_kernel,
        out_shape=[
            jax.ShapeDtypeStruct((share, units), jnp.float32),
            jax.ShapeDtypeStruct((4, share, units), jnp.bfloat16),
        ],
        in_specs=[SMEM, VMEM, VMEM],
        out_specs=[VMEM, VMEM],
        scratch_shapes=[pltpu.VMEM((4, share, units), jnp.float32)],
        compiler_params=pltpu.CompilerParams(vmem_limit_bytes=16 * MIB),
        cost_estimate=pl.CostEstimate(
            flops=16 * share * 1024 * units, bytes_accessed=8 * MIB, transcendentals=0
        ),
    )(y, gathered, swapped)


def shift(array, by):
    return lax.ppermute(array, "z", [(i, (i + by) % 4) for i in range(4)])


def local(
    layer_input,
    norm_gain,
    shift_mix,
    key_weight,
    value_weight,
    key_left,
    key_right,
    value_left,
    value_right,
    fitness_rank,
):
    members, units = key_right.shape
    z = lax.axis_index("z").astype(jnp.int32).reshape(1)
    core = lax.axis_index("core").astype(jnp.int32).reshape(1)
    gain, mix = norm_gain.reshape(1, D), shift_mix.reshape(1, D)
    rows, width = layer_input.shape[0] // 2, layer_input.shape[1]
    half = rows // 2

    inputs = []
    for c in range(2):
        own = layer_input[c * rows : (c + 1) * rows]
        top, bottom = own[:half], own[half:]
        if c == 0:
            left, right = shift(own, 1), shift(own, -1)
            left_top, left_bottom = left[:half], left[half:]
            right_top, right_bottom = right[:half], right[half:]
            pieces = [right, left]
        else:
            left_top, right_bottom = shift(top, 1), shift(bottom, -1)
            left_bottom, right_top = shift(bottom, 1), shift(top, -1)
            pieces = [right_top, left_top, right_bottom, left_bottom]
        pieces += [shift(left_top, 1), shift(right_bottom, -1)]
        inputs.append((own, pieces))

    weight = (fitness_rank.astype(jnp.float32) / (MEMBERS - 1) - 0.5) / math.sqrt(MEMBERS)
    length = D // 4 + units
    sent = pl.pallas_call(
        prepare_kernel,
        out_shape=jax.ShapeDtypeStruct((4, length, LANES), jnp.bfloat16),
        in_specs=[SMEM] + [VMEM] * 5 + [ANY],
        out_specs=VMEM,
        compiler_params=pltpu.CompilerParams(vmem_limit_bytes=8 * MIB),
        cost_estimate=pl.CostEstimate(flops=0, bytes_accessed=4 * MIB, transcendentals=0),
    )(core, weight[:, None], key_left, value_right, key_right, value_left, inputs[0][0])
    gathered = lax.all_to_all(sent, "x", split_axis=0, concat_axis=0, tiled=True)

    results = []
    for c, (own, pieces) in enumerate(inputs):
        part = slice(c * rows // PROMPT, (c + 1) * rows // PROMPT)
        results.append(
            ffn(
                z,
                own,
                pieces,
                gain * (1.0 - mix),
                gain * mix,
                key_weight,
                value_weight,
                key_left[part].astype(jnp.float32),
                key_right[part],
                value_left[part],
                value_right[part],
                place_after if c else z,
            )
        )
        if c == 0:
            swapped = gathered[:, D // 8 :]
            swapped = lax.ppermute(swapped, "core", [(0, 1), (1, 0)])
            update_own, update_parts = update_products(gathered, swapped, units)
            place_after = update_parts

    update_parts = lax.all_to_all(update_parts, "y", split_axis=0, concat_axis=0, tiled=True)
    update = sum(
        jnp.where(lax.axis_index("y") == y, update_own, update_parts[y].astype(jnp.float32))
        for y in range(4)
    )

    outputs = []
    for own, to_right, to_left, right_top, left_bottom in results:
        from_left, from_right = shift(to_right, 1), shift(to_left, -1)
        from_left_top = shift(right_top + from_left[:half], 1)
        from_right_bottom = shift(left_bottom + from_right[half:], -1)
        for mine, one, two in (
            (own[:half], from_left_top, from_right[:half]),
            (own[half:], from_left[half:], from_right_bottom),
        ):
            total = mine + (one.astype(jnp.float32) + two.astype(jnp.float32))
            outputs.append(total.astype(jnp.bfloat16))
    share = update.shape[0] // 2
    return (jnp.concatenate(outputs, axis=0), update[:share], update[share:].T)


def solution(mesh):
    mesh = Mesh(mesh.devices.reshape(4, 4, 2, 4), ("y", "x", "core", "z"))
    dp = ("y", "x", "core")
    placed = (
        P(dp, "z"),
        P(),
        P(),
        P(None, "z"),
        P("z", None),
        P(dp, None),
        P(dp, "z"),
        P(dp, "z"),
        P(dp, None),
        P(dp),
    )
    return jax.shard_map(
        local,
        mesh=mesh,
        in_specs=placed,
        out_specs=(P(dp, "z"), P(dp, "z"), P("z", dp)),
        check_vma=False,
    )
```

```python
import functools
import math

import jax
import jax.numpy as jnp
from jax import lax
from jax.experimental import pallas as pl
from jax.experimental.pallas import tpu as pltpu
from jax.sharding import Mesh, PartitionSpec as P

D = 2560
FFW = 5120
MEMBERS = 2048
PROMPT = 16
EPSILON = 1e-05
SIGMA = 0.5
KEY_FACTOR = SIGMA / math.sqrt(D)
VALUE_FACTOR = SIGMA / math.sqrt(FFW)
LN_ROWS = 64
F_BLOCK = 640
LANES = 128
MIB = 1024 * 1024

VMEM = pl.BlockSpec(memory_space=pltpu.VMEM)
SMEM = pl.BlockSpec(memory_space=pltpu.SMEM)
ANY = pl.BlockSpec(memory_space=pl.ANY)


def mm(a, b):
    return jnp.dot(a, b, preferred_element_type=jnp.float32)


def per_member(array, rows):
    members, width = array.shape
    wide = jnp.broadcast_to(array.astype(jnp.float32)[:, None, :], (members, PROMPT, width))
    return wide.reshape(rows, width)


def ffn_kernel(place, x0, *refs):
    pieces, refs = refs[:-20], refs[-20:]
    keep, pass_on, kw_hbm, vw_hbm, kl, kr, vl, vr, _, *refs = refs
    own, to_right, to_left, right_top, left_bottom, kw, vw, mixed, hidden, kdots, sems = refs
    rows, width = x0.shape
    half = rows // 2
    units = kw.shape[1]
    z = place[0]
    key_copy = pltpu.make_async_copy(kw_hbm, kw, sems.at[0])
    value_copy = pltpu.make_async_copy(vw_hbm, vw, sems.at[1])
    key_copy.start()
    value_copy.start()

    def column(k):
        return pl.multiple_of(lax.rem(z + k, 4) * width, 128)

    def normalise(i, sub, sources):
        first = pl.multiple_of(i * 128 + sub * LN_ROWS, LN_ROWS)
        span = pl.ds(first, LN_ROWS)
        group = pl.ds(pl.multiple_of(i * 8, 8), 8)
        ours = slice(sub * LN_ROWS // PROMPT, (sub + 1) * LN_ROWS // PROMPT)
        values = [x0[span, :]]
        for source, offset in sources:
            values.append(source[pl.ds(pl.multiple_of(first - offset, LN_ROWS), LN_ROWS), :])
        values = [v.astype(jnp.float32) for v in values]
        centre = sum(jnp.sum(v, axis=-1, keepdims=True) for v in values) * (1.0 / D)
        values = [v - centre for v in values]
        spread = sum(jnp.sum(v * v, axis=-1, keepdims=True) for v in values) * (1.0 / D)
        scale = lax.rsqrt(spread + EPSILON)
        later = lax.broadcasted_iota(jnp.int32, (LN_ROWS, 1), 0) % PROMPT != 0
        dots = 0.0
        for k, value in enumerate(values):
            cols = pl.ds(column(k), width)
            normed = value * scale
            before = pltpu.roll(normed * pass_on[:, cols], 1, 0)
            block = normed * keep[:, cols] + jnp.where(later, before, 0.0)
            block = block.astype(jnp.bfloat16)
            mixed[span, cols] = block
            left = per_member(kl[group, cols][ours], LN_ROWS)
            dots += jnp.sum(block.astype(jnp.float32) * left, axis=-1, keepdims=True)
        kdots[span, :] = dots * KEY_FACTOR

    def normalise_group(sources, i, carry):
        for sub in range(128 // LN_ROWS):
            normalise(i, sub, sources)
        return carry

    groups = rows // 128
    if len(pieces) == 4:
        right, left, far_top, far_bottom = pieces
        top, bottom = [(right, 0), (far_top, 0), (left, 0)], [(right, 0), (far_bottom, half), (left, 0)]
    else:
        near, far = pieces[:4], pieces[4:]
        top = [(near[0], 0), (far[0], 0), (near[1], 0)]
        bottom = [(near[2], half), (far[1], half), (near[3], half)]
    lax.fori_loop(0, groups // 2, functools.partial(normalise_group, top), 0)
    lax.fori_loop(groups // 2, groups, functools.partial(normalise_group, bottom), 0)

    key_copy.wait()
    vdots = 0.0
    for first in range(0, units, F_BLOCK):
        cols = pl.ds(first, F_BLOCK)
        preact = mm(mixed[...], kw[:, cols]) + kdots[...] * per_member(kr[:, cols], rows)
        block = jnp.square(jnp.maximum(preact, 0.0)).astype(jnp.bfloat16)
        hidden[:, cols] = block
        left = per_member(vl[:, cols], rows)
        vdots += jnp.sum(block.astype(jnp.float32) * left, axis=-1, keepdims=True)
    vdots = vdots * VALUE_FACTOR

    value_copy.wait()

    def sums(k):
        cols = pl.ds(column(k), width)
        return mm(hidden[...], vw[:, cols]) + vdots * per_member(vr[:, cols], rows)

    far = sums(2).astype(jnp.bfloat16)
    to_right[:half] = far[:half]
    to_left[half:] = far[half:]
    right = sums(1).astype(jnp.bfloat16)
    right_top[...] = right[:half]
    to_right[half:] = right[half:]
    left = sums(3).astype(jnp.bfloat16)
    to_left[:half] = left[:half]
    left_bottom[...] = left[half:]
    own[...] = sums(0)


def ffn(place, own, pieces, keep, pass_on, kw, vw, kl, kr, vl, vr, after):
    rows, width = own.shape
    units = kr.shape[1]
    half = rows // 2
    parts = [jax.ShapeDtypeStruct((n, width), jnp.bfloat16) for n in (rows, rows, half, half)]
    return pl.pallas_call(
        ffn_kernel,
        out_shape=[jax.ShapeDtypeStruct((rows, width), jnp.float32)] + parts,
        in_specs=[SMEM] + [VMEM] * (len(pieces) + 3) + [ANY] * 2 + [VMEM] * 4 + [ANY],
        out_specs=[VMEM] * 5,
        scratch_shapes=[
            pltpu.VMEM((D, units), jnp.bfloat16),
            pltpu.VMEM((units, D), jnp.bfloat16),
            pltpu.VMEM((rows, D), jnp.bfloat16),
            pltpu.VMEM((rows, units), jnp.bfloat16),
            pltpu.VMEM((rows, 1), jnp.float32),
            pltpu.SemaphoreType.DMA((2,)),
        ],
        compiler_params=pltpu.CompilerParams(vmem_limit_bytes=50 * MIB),
        cost_estimate=pl.CostEstimate(
            flops=16 * rows * D * units,
            bytes_accessed=4 * D * units + 8 * rows * D,
            transcendentals=rows,
        ),
    )(place, own, *pieces, keep, pass_on, kw, vw, kl, kr, vl, vr, after)


def prepare_kernel(place, weight, key_left, value_right, key_right, value_left, _, sent):
    core = place[0]
    rights = jnp.concatenate([key_right[...], value_left[...]], axis=0)
    scaled = [f[...].astype(jnp.float32) * weight[...] for f in (key_left, value_right)]
    lefts = jnp.concatenate([s.T for s in scaled], axis=1).astype(jnp.bfloat16)
    share = D // 32
    for x in range(4):
        for block in range(rights.shape[1] // LANES):
            rows = slice(4 * share + block * LANES, 4 * share + (block + 1) * LANES)
            sent[x, rows, :] = rights[:, block * LANES : (block + 1) * LANES]
        for c in range(2):
            first = jnp.where(core == c, 0, 4 * share + rights.shape[1])
            for y in range(4):
                start = ((y * 4 + x) * 2 + c) * share
                target = pl.ds(pl.multiple_of(first + y * share, 16), share)
                sent[x, target, :] = lefts[start : start + share]


def update_kernel(place, gathered, swapped, own, parts, sums):
    share, units = own.shape
    share //= 2
    lefts, rights = [], []
    for source, first_left, first_right in ((gathered, 0, 4 * share), (swapped, units, 0)):
        for x in range(4):
            lefts.append(source[x, first_left : first_left + 4 * share, :])
            blocks = range(first_right, first_right + units, LANES)
            rights.append(jnp.concatenate([source[x, b : b + LANES, :] for b in blocks], axis=1))
    rights = jnp.concatenate(rights, axis=0)
    lane = lax.broadcasted_iota(jnp.int32, lefts[0].shape, 1)
    for side in range(2):
        picked = [jnp.where((lane < LANES // 2) == (side == 0), b, 0.0) for b in lefts]
        total = mm(jnp.concatenate(picked, axis=1), rights)
        for y in range(4):
            sums[y, side * share : (side + 1) * share, :] = total[y * share : (y + 1) * share]
    own[...] = sums[place[0]]
    parts[...] = sums[...].astype(jnp.bfloat16)


def update_sum_kernel(place, own, parts, key_update, value_update):
    share = key_update.shape[0]
    for side, target in enumerate((key_update, value_update)):
        span = pl.ds(side * share, share)
        total = own[span, :]
        for y in range(4):
            total += jnp.where(place[0] == y, 0.0, parts[y, span, :].astype(jnp.float32))
        target[...] = total


def update_products(gathered, swapped, units):
    share = D // 16
    y = lax.axis_index("y").astype(jnp.int32).reshape(1)
    return pl.pallas_call(
        update_kernel,
        out_shape=[
            jax.ShapeDtypeStruct((share, units), jnp.float32),
            jax.ShapeDtypeStruct((4, share, units), jnp.bfloat16),
        ],
        in_specs=[SMEM, VMEM, VMEM],
        out_specs=[VMEM, VMEM],
        scratch_shapes=[pltpu.VMEM((4, share, units), jnp.float32)],
        compiler_params=pltpu.CompilerParams(vmem_limit_bytes=16 * MIB),
        cost_estimate=pl.CostEstimate(
            flops=16 * share * 1024 * units, bytes_accessed=8 * MIB, transcendentals=0
        ),
    )(y, gathered, swapped)


def shift(array, by):
    return lax.ppermute(array, "z", [(i, (i + by) % 4) for i in range(4)])


def local(
    layer_input,
    norm_gain,
    shift_mix,
    key_weight,
    value_weight,
    key_left,
    key_right,
    value_left,
    value_right,
    fitness_rank,
):
    members, units = key_right.shape
    z = lax.axis_index("z").astype(jnp.int32).reshape(1)
    core = lax.axis_index("core").astype(jnp.int32).reshape(1)
    gain, mix = norm_gain.reshape(1, D), shift_mix.reshape(1, D)
    rows, width = layer_input.shape[0] // 2, layer_input.shape[1]
    half = rows // 2

    inputs = []
    for c in range(2):
        own = layer_input[c * rows : (c + 1) * rows]
        top, bottom = own[:half], own[half:]
        if c == 0:
            left, right = shift(own, 1), shift(own, -1)
            left_top, left_bottom = left[:half], left[half:]
            right_top, right_bottom = right[:half], right[half:]
            pieces = [right, left]
        else:
            left_top, right_bottom = shift(top, 1), shift(bottom, -1)
            left_bottom, right_top = shift(bottom, 1), shift(top, -1)
            pieces = [right_top, left_top, right_bottom, left_bottom]
        pieces += [shift(left_top, 1), shift(right_bottom, -1)]
        inputs.append((own, pieces))

    weight = (fitness_rank.astype(jnp.float32) / (MEMBERS - 1) - 0.5) / math.sqrt(MEMBERS)
    length = D // 4 + units
    sent = pl.pallas_call(
        prepare_kernel,
        out_shape=jax.ShapeDtypeStruct((4, length, LANES), jnp.bfloat16),
        in_specs=[SMEM] + [VMEM] * 5 + [ANY],
        out_specs=VMEM,
        compiler_params=pltpu.CompilerParams(vmem_limit_bytes=8 * MIB),
        cost_estimate=pl.CostEstimate(flops=0, bytes_accessed=4 * MIB, transcendentals=0),
    )(core, weight[:, None], key_left, value_right, key_right, value_left, inputs[0][0])
    gathered = lax.all_to_all(sent, "x", split_axis=0, concat_axis=0, tiled=True)

    results = []
    for c, (own, pieces) in enumerate(inputs):
        part = slice(c * rows // PROMPT, (c + 1) * rows // PROMPT)
        results.append(
            ffn(
                z,
                own,
                pieces,
                gain * (1.0 - mix),
                gain * mix,
                key_weight,
                value_weight,
                key_left[part].astype(jnp.float32),
                key_right[part],
                value_left[part],
                value_right[part],
                place_after if c else z,
            )
        )
        if c == 0:
            swapped = gathered[:, D // 8 :]
            swapped = lax.ppermute(swapped, "core", [(0, 1), (1, 0)])
            update_own, update_parts = update_products(gathered, swapped, units)
            place_after = update_parts

    update_parts = lax.all_to_all(update_parts, "y", split_axis=0, concat_axis=0, tiled=True)
    y = lax.axis_index("y").astype(jnp.int32).reshape(1)
    share = update_own.shape[0] // 2
    key_update, value_update = pl.pallas_call(
        update_sum_kernel,
        out_shape=[jax.ShapeDtypeStruct((share, units), jnp.float32)] * 2,
        in_specs=[SMEM, VMEM, VMEM],
        out_specs=[VMEM] * 2,
        compiler_params=pltpu.CompilerParams(vmem_limit_bytes=6 * MIB),
        cost_estimate=pl.CostEstimate(flops=0, bytes_accessed=3 * MIB, transcendentals=0),
    )(y, update_own, update_parts)

    outputs = []
    for own, to_right, to_left, right_top, left_bottom in results:
        from_left, from_right = shift(to_right, 1), shift(to_left, -1)
        from_left_top = shift(right_top + from_left[:half], 1)
        from_right_bottom = shift(left_bottom + from_right[half:], -1)
        for mine, one, two in (
            (own[:half], from_left_top, from_right[:half]),
            (own[half:], from_left[half:], from_right_bottom),
        ):
            total = mine + (one.astype(jnp.float32) + two.astype(jnp.float32))
            outputs.append(total.astype(jnp.bfloat16))
    return (jnp.concatenate(outputs, axis=0), key_update, value_update.T)


def solution(mesh):
    mesh = Mesh(mesh.devices.reshape(4, 4, 2, 4), ("y", "x", "core", "z"))
    dp = ("y", "x", "core")
    placed = (
        P(dp, "z"),
        P(),
        P(),
        P(None, "z"),
        P("z", None),
        P(dp, None),
        P(dp, "z"),
        P(dp, "z"),
        P(dp, None),
        P(dp),
    )
    return jax.shard_map(
        local,
        mesh=mesh,
        in_specs=placed,
        out_specs=(P(dp, "z"), P(dp, "z"), P("z", dp)),
        check_vma=False,
    )
```

```python
import functools
import math

import jax
import jax.numpy as jnp
from jax import lax
from jax.experimental import pallas as pl
from jax.experimental.pallas import tpu as pltpu
from jax.sharding import Mesh, PartitionSpec as P

D = 2560
FFW = 5120
MEMBERS = 2048
PROMPT = 16
EPSILON = 1e-05
SIGMA = 0.5
KEY_FACTOR = SIGMA / math.sqrt(D)
VALUE_FACTOR = SIGMA / math.sqrt(FFW)
LN_ROWS = 64
F_BLOCK = 640
LANES = 128
MIB = 1024 * 1024

VMEM = pl.BlockSpec(memory_space=pltpu.VMEM)
SMEM = pl.BlockSpec(memory_space=pltpu.SMEM)
ANY = pl.BlockSpec(memory_space=pl.ANY)


def mm(a, b):
    return jnp.dot(a, b, preferred_element_type=jnp.float32)


def per_member(array, rows):
    members, width = array.shape
    wide = jnp.broadcast_to(array.astype(jnp.float32)[:, None, :], (members, PROMPT, width))
    return wide.reshape(rows, width)


def ffn_kernel(place, x0, *refs):
    pieces, refs = refs[:-20], refs[-20:]
    keep, pass_on, kw_hbm, vw_hbm, kl, kr, vl, vr, _, *refs = refs
    own, to_right, to_left, right_top, left_bottom, kw, vw, mixed, hidden, kdots, sems = refs
    rows, width = x0.shape
    half = rows // 2
    units = kw.shape[1]
    z = place[0]
    key_copy = pltpu.make_async_copy(kw_hbm, kw, sems.at[0])
    value_copy = pltpu.make_async_copy(vw_hbm, vw, sems.at[1])
    key_copy.start()

    def column(k):
        return pl.multiple_of(lax.rem(z + k, 4) * width, 128)

    def normalise(i, sub, sources):
        first = pl.multiple_of(i * 128 + sub * LN_ROWS, LN_ROWS)
        span = pl.ds(first, LN_ROWS)
        group = pl.ds(pl.multiple_of(i * 8, 8), 8)
        ours = slice(sub * LN_ROWS // PROMPT, (sub + 1) * LN_ROWS // PROMPT)
        values = [x0[span, :]]
        for source, offset in sources:
            values.append(source[pl.ds(pl.multiple_of(first - offset, LN_ROWS), LN_ROWS), :])
        values = [v.astype(jnp.float32) for v in values]
        centre = sum(jnp.sum(v, axis=-1, keepdims=True) for v in values) * (1.0 / D)
        values = [v - centre for v in values]
        spread = sum(jnp.sum(v * v, axis=-1, keepdims=True) for v in values) * (1.0 / D)
        scale = lax.rsqrt(spread + EPSILON)
        later = lax.broadcasted_iota(jnp.int32, (LN_ROWS, 1), 0) % PROMPT != 0
        dots = 0.0
        for k, value in enumerate(values):
            cols = pl.ds(column(k), width)
            normed = value * scale
            before = pltpu.roll(normed * pass_on[:, cols], 1, 0)
            block = normed * keep[:, cols] + jnp.where(later, before, 0.0)
            block = block.astype(jnp.bfloat16)
            mixed[span, cols] = block
            left = per_member(kl[group, cols][ours], LN_ROWS)
            dots += jnp.sum(block.astype(jnp.float32) * left, axis=-1, keepdims=True)
        kdots[span, :] = dots * KEY_FACTOR

    def normalise_group(sources, i, carry):
        for sub in range(128 // LN_ROWS):
            normalise(i, sub, sources)
        return carry

    groups = rows // 128
    if len(pieces) == 4:
        right, left, far_top, far_bottom = pieces
        top, bottom = [(right, 0), (far_top, 0), (left, 0)], [(right, 0), (far_bottom, half), (left, 0)]
    else:
        near, far = pieces[:4], pieces[4:]
        top = [(near[0], 0), (far[0], 0), (near[1], 0)]
        bottom = [(near[2], half), (far[1], half), (near[3], half)]
    lax.fori_loop(0, groups // 2, functools.partial(normalise_group, top), 0)
    value_copy.start()
    lax.fori_loop(groups // 2, groups, functools.partial(normalise_group, bottom), 0)

    key_copy.wait()
    vdots = 0.0
    for first in range(0, units, F_BLOCK):
        cols = pl.ds(first, F_BLOCK)
        preact = mm(mixed[...], kw[:, cols]) + kdots[...] * per_member(kr[:, cols], rows)
        block = jnp.square(jnp.maximum(preact, 0.0)).astype(jnp.bfloat16)
        hidden[:, cols] = block
        left = per_member(vl[:, cols], rows)
        vdots += jnp.sum(block.astype(jnp.float32) * left, axis=-1, keepdims=True)
    vdots = vdots * VALUE_FACTOR

    value_copy.wait()

    def sums(k):
        cols = pl.ds(column(k), width)
        return mm(hidden[...], vw[:, cols]) + vdots * per_member(vr[:, cols], rows)

    far = sums(2).astype(jnp.bfloat16)
    to_right[:half] = far[:half]
    to_left[half:] = far[half:]
    right = sums(1).astype(jnp.bfloat16)
    right_top[...] = right[:half]
    to_right[half:] = right[half:]
    left = sums(3).astype(jnp.bfloat16)
    to_left[:half] = left[:half]
    left_bottom[...] = left[half:]
    own[...] = sums(0)


def ffn(place, own, pieces, keep, pass_on, kw, vw, kl, kr, vl, vr, after):
    rows, width = own.shape
    units = kr.shape[1]
    half = rows // 2
    parts = [jax.ShapeDtypeStruct((n, width), jnp.bfloat16) for n in (rows, rows, half, half)]
    return pl.pallas_call(
        ffn_kernel,
        out_shape=[jax.ShapeDtypeStruct((rows, width), jnp.float32)] + parts,
        in_specs=[SMEM] + [VMEM] * (len(pieces) + 3) + [ANY] * 2 + [VMEM] * 4 + [ANY],
        out_specs=[VMEM] * 5,
        scratch_shapes=[
            pltpu.VMEM((D, units), jnp.bfloat16),
            pltpu.VMEM((units, D), jnp.bfloat16),
            pltpu.VMEM((rows, D), jnp.bfloat16),
            pltpu.VMEM((rows, units), jnp.bfloat16),
            pltpu.VMEM((rows, 1), jnp.float32),
            pltpu.SemaphoreType.DMA((2,)),
        ],
        compiler_params=pltpu.CompilerParams(vmem_limit_bytes=50 * MIB),
        cost_estimate=pl.CostEstimate(
            flops=16 * rows * D * units,
            bytes_accessed=4 * D * units + 8 * rows * D,
            transcendentals=rows,
        ),
    )(place, own, *pieces, keep, pass_on, kw, vw, kl, kr, vl, vr, after)


def prepare_kernel(place, weight, key_left, value_right, key_right, value_left, _, sent):
    core = place[0]
    rights = jnp.concatenate([key_right[...], value_left[...]], axis=0)
    scaled = [f[...].astype(jnp.float32) * weight[...] for f in (key_left, value_right)]
    lefts = jnp.concatenate([s.T for s in scaled], axis=1).astype(jnp.bfloat16)
    share = D // 32
    for x in range(4):
        for block in range(rights.shape[1] // LANES):
            rows = slice(4 * share + block * LANES, 4 * share + (block + 1) * LANES)
            sent[x, rows, :] = rights[:, block * LANES : (block + 1) * LANES]
        for c in range(2):
            first = jnp.where(core == c, 0, 4 * share + rights.shape[1])
            for y in range(4):
                start = ((y * 4 + x) * 2 + c) * share
                target = pl.ds(pl.multiple_of(first + y * share, 16), share)
                sent[x, target, :] = lefts[start : start + share]


def update_kernel(place, gathered, swapped, own, parts, sums):
    share, units = own.shape
    share //= 2
    lefts, rights = [], []
    for source, first_left, first_right in ((gathered, 0, 4 * share), (swapped, units, 0)):
        for x in range(4):
            lefts.append(source[x, first_left : first_left + 4 * share, :])
            blocks = range(first_right, first_right + units, LANES)
            rights.append(jnp.concatenate([source[x, b : b + LANES, :] for b in blocks], axis=1))
    rights = jnp.concatenate(rights, axis=0)
    lane = lax.broadcasted_iota(jnp.int32, lefts[0].shape, 1)
    for side in range(2):
        picked = [jnp.where((lane < LANES // 2) == (side == 0), b, 0.0) for b in lefts]
        total = mm(jnp.concatenate(picked, axis=1), rights)
        for y in range(4):
            sums[y, side * share : (side + 1) * share, :] = total[y * share : (y + 1) * share]
    own[...] = sums[place[0]]
    parts[...] = sums[...].astype(jnp.bfloat16)


def update_sum_kernel(place, own, parts, key_update, value_update):
    share = key_update.shape[0]
    for side, target in enumerate((key_update, value_update)):
        span = pl.ds(side * share, share)
        total = own[span, :]
        for y in range(4):
            total += jnp.where(place[0] == y, 0.0, parts[y, span, :].astype(jnp.float32))
        target[...] = total


def update_products(gathered, swapped, units):
    share = D // 16
    y = lax.axis_index("y").astype(jnp.int32).reshape(1)
    return pl.pallas_call(
        update_kernel,
        out_shape=[
            jax.ShapeDtypeStruct((share, units), jnp.float32),
            jax.ShapeDtypeStruct((4, share, units), jnp.bfloat16),
        ],
        in_specs=[SMEM, VMEM, VMEM],
        out_specs=[VMEM, VMEM],
        scratch_shapes=[pltpu.VMEM((4, share, units), jnp.float32)],
        compiler_params=pltpu.CompilerParams(vmem_limit_bytes=16 * MIB),
        cost_estimate=pl.CostEstimate(
            flops=16 * share * 1024 * units, bytes_accessed=8 * MIB, transcendentals=0
        ),
    )(y, gathered, swapped)


def shift(array, by):
    return lax.ppermute(array, "z", [(i, (i + by) % 4) for i in range(4)])


def local(
    layer_input,
    norm_gain,
    shift_mix,
    key_weight,
    value_weight,
    key_left,
    key_right,
    value_left,
    value_right,
    fitness_rank,
):
    members, units = key_right.shape
    z = lax.axis_index("z").astype(jnp.int32).reshape(1)
    core = lax.axis_index("core").astype(jnp.int32).reshape(1)
    gain, mix = norm_gain.reshape(1, D), shift_mix.reshape(1, D)
    rows, width = layer_input.shape[0] // 2, layer_input.shape[1]
    half = rows // 2

    inputs = []
    for c in range(2):
        own = layer_input[c * rows : (c + 1) * rows]
        top, bottom = own[:half], own[half:]
        if c == 0:
            left, right = shift(own, 1), shift(own, -1)
            left_top, left_bottom = left[:half], left[half:]
            right_top, right_bottom = right[:half], right[half:]
            pieces = [right, left]
        else:
            left_top, right_bottom = shift(top, 1), shift(bottom, -1)
            left_bottom, right_top = shift(bottom, 1), shift(top, -1)
            pieces = [right_top, left_top, right_bottom, left_bottom]
        pieces += [shift(left_top, 1), shift(right_bottom, -1)]
        inputs.append((own, pieces))

    weight = (fitness_rank.astype(jnp.float32) / (MEMBERS - 1) - 0.5) / math.sqrt(MEMBERS)
    length = D // 4 + units
    sent = pl.pallas_call(
        prepare_kernel,
        out_shape=jax.ShapeDtypeStruct((4, length, LANES), jnp.bfloat16),
        in_specs=[SMEM] + [VMEM] * 5 + [ANY],
        out_specs=VMEM,
        compiler_params=pltpu.CompilerParams(vmem_limit_bytes=8 * MIB),
        cost_estimate=pl.CostEstimate(flops=0, bytes_accessed=4 * MIB, transcendentals=0),
    )(core, weight[:, None], key_left, value_right, key_right, value_left, inputs[0][0])
    gathered = lax.all_to_all(sent, "x", split_axis=0, concat_axis=0, tiled=True)

    results = []
    for c, (own, pieces) in enumerate(inputs):
        part = slice(c * rows // PROMPT, (c + 1) * rows // PROMPT)
        results.append(
            ffn(
                z,
                own,
                pieces,
                gain * (1.0 - mix),
                gain * mix,
                key_weight,
                value_weight,
                key_left[part].astype(jnp.float32),
                key_right[part],
                value_left[part],
                value_right[part],
                place_after if c else z,
            )
        )
        if c == 0:
            swapped = gathered[:, D // 8 :]
            swapped = lax.ppermute(swapped, "core", [(0, 1), (1, 0)])
            update_own, update_parts = update_products(gathered, swapped, units)
            place_after = update_parts

    update_parts = lax.all_to_all(update_parts, "y", split_axis=0, concat_axis=0, tiled=True)
    y = lax.axis_index("y").astype(jnp.int32).reshape(1)
    share = update_own.shape[0] // 2
    key_update, value_update = pl.pallas_call(
        update_sum_kernel,
        out_shape=[jax.ShapeDtypeStruct((share, units), jnp.float32)] * 2,
        in_specs=[SMEM, VMEM, VMEM],
        out_specs=[VMEM] * 2,
        compiler_params=pltpu.CompilerParams(vmem_limit_bytes=6 * MIB),
        cost_estimate=pl.CostEstimate(flops=0, bytes_accessed=3 * MIB, transcendentals=0),
    )(y, update_own, update_parts)

    outputs = []
    for own, to_right, to_left, right_top, left_bottom in results:
        from_left, from_right = shift(to_right, 1), shift(to_left, -1)
        from_left_top = shift(right_top + from_left[:half], 1)
        from_right_bottom = shift(left_bottom + from_right[half:], -1)
        for mine, one, two in (
            (own[:half], from_left_top, from_right[:half]),
            (own[half:], from_left[half:], from_right_bottom),
        ):
            total = mine + (one.astype(jnp.float32) + two.astype(jnp.float32))
            outputs.append(total.astype(jnp.bfloat16))
    return (jnp.concatenate(outputs, axis=0), key_update, value_update.T)


def solution(mesh):
    mesh = Mesh(mesh.devices.reshape(4, 4, 2, 4), ("y", "x", "core", "z"))
    dp = ("y", "x", "core")
    placed = (
        P(dp, "z"),
        P(),
        P(),
        P(None, "z"),
        P("z", None),
        P(dp, None),
        P(dp, "z"),
        P(dp, "z"),
        P(dp, None),
        P(dp),
    )
    return jax.shard_map(
        local,
        mesh=mesh,
        in_specs=placed,
        out_specs=(P(dp, "z"), P(dp, "z"), P("z", dp)),
        check_vma=False,
    )
```
